512 devices in a mesh: dp: 64 (over z_hi, y, x, core), tensor: 8 (over z_lo).
Axes of the slice: x: 4, y: 4, z: 16 (z_hi: 2, z_lo: 8; z = z_hi * 8 + z_lo), core: 2. Of those that a mesh axis runs over, the one named last changes fastest.
Arguments:
- queries: bfloat16 [8192, 8192], P('dp', 'tensor'), may hold values from -32 to 32
- key_value_store: bfloat16 [128, 1600, 2048], P('dp', 'tensor'), may hold values from -24 to 24
- output_gradient: bfloat16 [8192, 8192], P('dp', 'tensor'), may hold values from -6 to 6
- image_ids: int32 [64, 4], replicated, may hold values from 0 to 127, as said below
- image_counts: int32 [64], replicated, may hold values from 0 to 4, as said below
- image_start: int32 [64, 4], replicated, may hold values from 0 to 128, as said below
Outputs:
- attended: bfloat16 [8192, 8192], P('dp', 'tensor')
- grad_queries: bfloat16 [8192, 8192], P('dp', 'tensor')
- grad_kv: bfloat16 [128, 1600, 2048], P('dp', 'tensor')
The draws below stay inside these ranges and needn't reach their ends.
Inputs may be any that keep to these rules, and one draw needn't show every extreme that they name: `image_ids`: slot m of sample s names an image for m < image_counts[s]; every image is named by exactly one such slot. Device d of dp owns images d * 2 to (d + 1) * 2 - 1, and an image named by sample s is owned by device s or device (s + 1) modulo 64. Entries at or past a sample's count name some image and are unused. `image_counts`: the counts sum to 128; some sample has 4 images and some has none. `image_start`: within a sample the starts rise strictly with the slot; entries at or past the count are 128.
All inputs are finite; a program needn't handle non-finite values.
Results may differ from the reference program's by a relative error of at most 0.012.
Values may be sent and summed in bfloat16 or wider, within the bound.
No kernel may reach another device: no remote copies, remote signals or barrier semaphores. Data moves between devices by JAX's collectives and lax.ppermute only.
A program may use at most 64 MiB of HBM per device.

```python
import math
import jax
import jax.numpy as jnp
from jax import lax

QUERY_HEADS = 64
KEY_VALUE_HEADS = 8
HEAD_DIM_SIZE = 128
VISION_TOKENS = 1600
IMG_DEV = 2
MAX_IMAGES = 4
TOKENS_PER_SHARD = 128
SAMPLE_TOTAL = 64
TOKENS = 8192
IMAGE_TOTAL = 128


def spread_scale(key, shape, lower, upper):
    return jnp.exp(jax.random.uniform(key, shape, jnp.float32, math.log(lower), math.log(upper)))


def routing(key):
    key_extra, key_anchor, key_turn, key_first, key_steps = jax.random.split(key, 5)
    sample_axis = jnp.arange(SAMPLE_TOTAL, dtype=jnp.int32)
    extra = jax.random.randint(key_extra, (SAMPLE_TOTAL,), 0, IMG_DEV + 1)
    anchor = jax.random.randint(key_anchor, (), 0, SAMPLE_TOTAL)
    offset = (sample_axis - anchor) % SAMPLE_TOTAL
    extra = jnp.where(offset == 0, 0, jnp.where(offset == 1, IMG_DEV, jnp.where(offset == 2, 0, extra)))
    following = jnp.roll(extra, -1)
    counts = IMG_DEV + following - extra
    first_image = sample_axis * IMG_DEV + extra
    slot_axis = jnp.arange(MAX_IMAGES, dtype=jnp.int32)
    flat = (first_image[:, None] + slot_axis[None, :]) % IMAGE_TOTAL
    owner = flat // IMG_DEV
    turn = jax.random.randint(key_turn, (SAMPLE_TOTAL,), 0, IMG_DEV)
    ids = owner * IMG_DEV + (flat % IMG_DEV + turn[owner]) % IMG_DEV
    is_used = slot_axis[None, :] < counts[:, None]
    first_start = jax.random.randint(key_first, (SAMPLE_TOTAL, 1), 0, TOKENS_PER_SHARD // 4)
    steps_up = jax.random.randint(key_steps, (SAMPLE_TOTAL, MAX_IMAGES), 1, TOKENS_PER_SHARD // 4 + 1)
    starts = first_start + jnp.cumsum(steps_up, axis=1) - steps_up[:, :1]
    starts = jnp.where(is_used, starts, TOKENS_PER_SHARD)
    return (ids.astype(jnp.int32), counts.astype(jnp.int32), starts.astype(jnp.int32))


def draw_image_ids(key, part):
    shared = routing(key)
    return shared[0]


def draw_image_counts(key, part):
    shared = routing(key)
    return shared[1]


def draw_image_start(key, part):
    shared = routing(key)
    return shared[2]


def draw_queries(key, part):
    key = jax.random.fold_in(key, 11)
    key_base, key_scale = jax.random.split(key, 2)
    noise = jax.random.truncated_normal(key_base, -6.0, 6.0, (TOKENS, QUERY_HEADS, HEAD_DIM_SIZE), jnp.float32)
    values = noise * spread_scale(key_scale, (TOKENS, QUERY_HEADS, 1), 0.3, 3.0)
    return jnp.clip(values, -32.0, 32.0).reshape(TOKENS, QUERY_HEADS * HEAD_DIM_SIZE).astype(jnp.bfloat16)


def draw_key_value_store(key, part):
    key = jax.random.fold_in(key, 23)
    random_key_for_keys, key_scale, random_key_for_values = jax.random.split(key, 3)
    key_matrix_rows = jax.random.truncated_normal(random_key_for_keys, -6.0, 6.0, (IMAGE_TOTAL, VISION_TOKENS, KEY_VALUE_HEADS, HEAD_DIM_SIZE), jnp.float32)
    key_matrix_rows = key_matrix_rows * spread_scale(key_scale, (IMAGE_TOTAL, VISION_TOKENS, 1, 1), 0.3, 3.0)
    value_matrix_rows = jax.random.truncated_normal(random_key_for_values, -6.0, 6.0, (IMAGE_TOTAL, VISION_TOKENS, KEY_VALUE_HEADS, HEAD_DIM_SIZE), jnp.float32)
    stacked_arrays = jnp.stack([key_matrix_rows, value_matrix_rows], axis=3)
    return jnp.clip(stacked_arrays, -24.0, 24.0).reshape(IMAGE_TOTAL, VISION_TOKENS, KEY_VALUE_HEADS * 2 * HEAD_DIM_SIZE).astype(jnp.bfloat16)


def level_of(key, shape, cuts, least, largest):
    gain, own = 1.0, jax.random.fold_in(key, 6)
    for dim, parts in cuts:
        steps = jnp.exp(jax.random.uniform(jax.random.fold_in(own, dim), (parts,), jnp.float32, least / len(cuts), largest / len(cuts)))
        gain = gain * jnp.repeat(steps, shape[dim] // parts).reshape([-1 if axis == dim else 1 for axis in range(len(shape))])
    return gain


def centred(stream_key, dims, width, bound, shards=(), held_as=jnp.bfloat16):
    entries = jax.random.normal(stream_key, dims, jnp.float32) * width
    if len(shards) > 0:
        entries = level_of(stream_key, dims, shards, -0.22, 0.18) * entries
    return jnp.clip(entries, min=-bound, max=bound).astype(held_as)


def setup_inputs(seed: int = 0) -> dict:
    key_of = jax.random.split(jax.random.key(seed), 7)
    return {
        "queries": draw_queries(jax.random.fold_in(key_of[6], 71), 0),
        "key_value_store": draw_key_value_store(jax.random.fold_in(key_of[6], 71), 0),
        "output_gradient": centred(key_of[2], (TOKENS, QUERY_HEADS * HEAD_DIM_SIZE), 1.0, 6.0, ((0, 64), (1, 8))),
        "image_ids": draw_image_ids(jax.random.fold_in(key_of[6], 71), 0),
        "image_counts": draw_image_counts(jax.random.fold_in(key_of[6], 71), 0),
        "image_start": draw_image_start(jax.random.fold_in(key_of[6], 71), 0),
    }


NEG_FILL = -1.0e30


def reference(queries, key_value_store, output_gradient, image_ids, image_counts, image_start):
    score_scale = HEAD_DIM_SIZE ** -0.5
    group_width = QUERY_HEADS // KEY_VALUE_HEADS
    query_parts = queries.reshape(SAMPLE_TOTAL, TOKENS_PER_SHARD, KEY_VALUE_HEADS, group_width, HEAD_DIM_SIZE)
    cotangent_parts = output_gradient.reshape(SAMPLE_TOTAL, TOKENS_PER_SHARD, KEY_VALUE_HEADS, group_width, HEAD_DIM_SIZE)
    store_parts = key_value_store.reshape(IMAGE_TOTAL, VISION_TOKENS, KEY_VALUE_HEADS, 2, HEAD_DIM_SIZE)
    positions = jnp.arange(TOKENS_PER_SHARD, dtype=jnp.int32)
    slot_axis = jnp.arange(MAX_IMAGES, dtype=jnp.int32)

    def one_sample(state, inputs):
        query_s, cot_s, ids_s, count_s, start_s = inputs
        chosen = store_parts[ids_s.astype(jnp.int32)]
        is_live = slot_axis < count_s
        visible = is_live[None, :] & (positions[:, None] >= start_s[None, :])
        visible_wide = visible[:, None, :, None]

        def one_group(group_inputs):
            query_g, cot_g, key_matrix_rows, value_matrix_rows = group_inputs
            query_f = query_g.astype(jnp.float32)
            cot_f = cot_g.astype(jnp.float32)
            key_f = key_matrix_rows.astype(jnp.float32)
            value_f = value_matrix_rows.astype(jnp.float32)
            scores = jnp.einsum("thd,mvd->thmv", query_f, key_f) * score_scale
            row_top = jnp.max(jnp.where(visible_wide, scores, NEG_FILL), axis=(2, 3))
            row_total = jnp.sum(jnp.where(visible_wide, jnp.exp(scores - row_top[..., None, None]), 0.0), axis=(2, 3))
            log_total = jnp.where(row_total > 0.0, row_top + jnp.log(jnp.maximum(row_total, 1.0)), 0.0)
            weights = jnp.where(visible_wide, jnp.exp(scores - log_total[..., None, None]), 0.0)
            weights_half = weights.astype(jnp.bfloat16).astype(jnp.float32)
            attended = jnp.einsum("thmv,mvd->thd", weights_half, value_f).astype(jnp.bfloat16)
            delta_row = jnp.sum(cot_f * attended.astype(jnp.float32), axis=2)
            dweights = jnp.einsum("thd,mvd->thmv", cot_f, value_f)
            dscores = (weights * (dweights - delta_row[..., None, None])).astype(jnp.bfloat16).astype(jnp.float32)
            dquery = (jnp.einsum("thmv,mvd->thd", dscores, key_f) * score_scale).astype(jnp.bfloat16)
            dkey_rows = jnp.einsum("thmv,thd->mvd", dscores, query_f) * score_scale
            dvalue_rows = jnp.einsum("thmv,thd->mvd", weights_half, cot_f)
            grads = jnp.stack([dkey_rows, dvalue_rows], axis=2).astype(jnp.bfloat16)
            return attended, dquery, grads

        attended_g, dquery_g, gradients_general = lax.map(one_group, (
            query_s.transpose(1, 0, 2, 3),
            cot_s.transpose(1, 0, 2, 3),
            chosen[:, :, :, 0].transpose(2, 0, 1, 3),
            chosen[:, :, :, 1].transpose(2, 0, 1, 3)))
        attended_s = attended_g.transpose(1, 0, 2, 3).reshape(TOKENS_PER_SHARD, QUERY_HEADS * HEAD_DIM_SIZE)
        dquery_s = dquery_g.transpose(1, 0, 2, 3).reshape(TOKENS_PER_SHARD, QUERY_HEADS * HEAD_DIM_SIZE)
        gradients_special = gradients_general.transpose(1, 2, 0, 3, 4).reshape(MAX_IMAGES, VISION_TOKENS, KEY_VALUE_HEADS * 2 * HEAD_DIM_SIZE)
        gradients_special = jnp.where(is_live[:, None, None], gradients_special, jnp.zeros_like(gradients_special))
        state = state.at[ids_s.astype(jnp.int32)].add(gradients_special)
        return state, (attended_s, dquery_s)

    initial_state = jnp.zeros((IMAGE_TOTAL, VISION_TOKENS, KEY_VALUE_HEADS * 2 * HEAD_DIM_SIZE), jnp.bfloat16)
    grad_kv, (attended, grad_queries) = lax.scan(
        one_sample, initial_state, (query_parts, cotangent_parts, image_ids, image_counts, image_start))
    return attended.reshape(TOKENS, QUERY_HEADS * HEAD_DIM_SIZE), grad_queries.reshape(TOKENS, QUERY_HEADS * HEAD_DIM_SIZE), grad_kv
```

```python
import functools
import math

import jax
import jax.numpy as jnp
from jax import lax
from jax.experimental import pallas as pl
from jax.experimental.pallas import tpu as pltpu
from jax.sharding import PartitionSpec as P

HEAD = 128
IMG_DEV = 2
NEG_FILL = -1e30
BIG = 1e30
LOG2E = 1.4426950408889634
SCALE = HEAD ** (-0.5)
SCALE2 = SCALE * LOG2E

NT = (((1,), (1,)), ((), ()))
TN = (((0,), (0,)), ((), ()))
NN = (((1,), (0,)), ((), ()))


def dot(a, b, dims):
    return lax.dot_general(a, b, dims, preferred_element_type=jnp.float32)


def shift(value, axis, steps):
    count = lax.axis_size(axis)
    pairs = [(source, (source + steps) % count) for source in range(count)]
    return lax.ppermute(value, axis, pairs)


def stack_heads(src_ref, dst_ref, slot):
    rows, cols = src_ref.shape
    for h in range(cols // HEAD):
        dst_ref[slot, h * rows : (h + 1) * rows, :] = src_ref[:, h * HEAD : (h + 1) * HEAD]


def visible_rows(start, rows, width):
    pos = lax.broadcasted_iota(jnp.int32, (1, width), 1) % rows
    return pos >= start


def fwd_kernel(meta, q_own, q_back, g_own, g_back, kv, o_own, o_back, stats, qr, gr, score, wts, acc):
    tok, cols = q_own.shape
    width = tok * cols // HEAD
    keys = kv.shape[1]
    tile = score.shape[0] // 4
    stack_heads(q_own, qr, 0)
    stack_heads(q_back, qr, 1)
    stack_heads(g_own, gr, 0)
    stack_heads(g_back, gr, 1)
    acc[...] = jnp.zeros_like(acc)
    stats[...] = jnp.zeros_like(stats)
    for slot in range(2):
        stats[slot, 0:1, :] = jnp.full((1, width), NEG_FILL, jnp.float32)
    for img in range(IMG_DEV):
        slot = meta[img, 0]
        seen = visible_rows(meta[img, 1], tok, width)
        top = jnp.full((1, width), NEG_FILL, jnp.float32)
        for step in range(keys // tile):
            rows = slice(step * tile, (step + 1) * tile)
            part = dot(kv[img, rows, :HEAD], qr[slot], NT)
            score[rows, :] = part
            top = jnp.maximum(top, jnp.max(part, axis=0, keepdims=True))
        total = jnp.zeros((1, width), jnp.float32)
        out = jnp.zeros((HEAD, width), jnp.float32)
        for step in range(keys // tile):
            rows = slice(step * tile, (step + 1) * tile)
            part = jnp.exp2((score[rows, :] - top) * SCALE2)
            total = total + jnp.sum(part, axis=0, keepdims=True)
            out = out + dot(kv[img, rows, HEAD:], part.astype(jnp.bfloat16), TN)
        old_top = stats[slot, 0:1, :]
        top = jnp.where(seen, top, NEG_FILL)
        new_top = jnp.maximum(old_top, top)
        old_w = jnp.exp2((old_top - new_top) * SCALE2)
        new_w = jnp.where(seen, jnp.exp2((top - new_top) * SCALE2), 0.0)
        stats[slot, 0:1, :] = new_top
        stats[slot, 1:2, :] = stats[slot, 1:2, :] * old_w + total * new_w
        acc[slot] = acc[slot] * old_w + out * new_w
    eye = (
        lax.broadcasted_iota(jnp.int32, (HEAD, HEAD), 0)
        == lax.broadcasted_iota(jnp.int32, (HEAD, HEAD), 1)
    ).astype(jnp.bfloat16)
    for slot in range(2):
        total = stats[slot, 1:2, :]
        mean = acc[slot] * jnp.where(total > 0.0, 1.0 / jnp.maximum(total, 1e-30), 0.0)
        cot = dot(eye, gr[slot], NT)
        stats[slot, 2:3, :] = jnp.sum(cot * mean, axis=0, keepdims=True)
        if slot == 0:
            o_own[...] = mean
        else:
            o_back[...] = mean.astype(jnp.bfloat16)


def merge(first, second):
    top = jnp.maximum(first[0:1], second[0:1])
    w_first = first[1:2] * jnp.exp2((first[0:1] - top) * SCALE2)
    w_second = second[1:2] * jnp.exp2((second[0:1] - top) * SCALE2)
    total = w_first + w_second
    inv = jnp.where(total > 0.0, 1.0 / jnp.maximum(total, 1e-30), 0.0)
    return top, total, w_first * inv, w_second * inv


def bwd_kernel(meta, q_own, q_back, g_own, g_back, kv, stats, far_own, far_back,
               dq_own, dq_back, dkv, qr, gr, acc):
    tok, cols = q_own.shape
    width = tok * cols // HEAD
    keys = kv.shape[1]
    tile = 400 if keys % 400 == 0 else keys
    stack_heads(q_own, qr, 0)
    stack_heads(q_back, qr, 1)
    stack_heads(g_own, gr, 0)
    stack_heads(g_back, gr, 1)
    acc[...] = jnp.zeros_like(acc)
    logs, deltas = [], []
    for slot, far in ((0, far_own), (1, far_back)):
        near_v = stats[slot]
        far_v = far[...]
        top, total, w_near, w_far = merge(near_v, far_v)
        logs.append(jnp.where(total > 0.0, top * SCALE2 + jnp.log(jnp.maximum(total, 1e-30)) * LOG2E, 0.0))
        deltas.append(w_near * near_v[2:3] + w_far * far_v[2:3])
    for img in range(IMG_DEV):
        slot = meta[img, 0]
        seen = visible_rows(meta[img, 1], tok, width)
        log_total = jnp.where(slot == 0, logs[0], logs[1])
        log_total = jnp.where(seen, log_total, BIG)
        delta = jnp.where(slot == 0, deltas[0], deltas[1])
        for step in range(keys // tile):
            rows = slice(step * tile, (step + 1) * tile)
            key = kv[img, rows, :HEAD]
            part = jnp.exp2(dot(key, qr[slot], NT) * SCALE2 - log_total)
            dweight = dot(kv[img, rows, HEAD:], gr[slot], NT)
            ds = (part * (dweight - delta)).astype(jnp.bfloat16)
            dkv[img, rows, HEAD:] = dot(part.astype(jnp.bfloat16), gr[slot], NN).astype(jnp.bfloat16)
            dkv[img, rows, :HEAD] = (dot(ds, qr[slot], NN) * SCALE).astype(jnp.bfloat16)
            acc[slot] = acc[slot] + dot(key, ds, TN)
    for slot, out in ((0, dq_own), (1, dq_back)):
        for h in range(cols // HEAD):
            block = acc[slot, :, h * tok : (h + 1) * tok] * SCALE
            out[:, h * HEAD : (h + 1) * HEAD] = block.T.astype(out.dtype)


def finish_kernel(o_own, o_far, stats, far, out):
    tok, cols = out.shape
    _, _, w_near, w_far = merge(stats[0], far[...])
    whole = o_own[...] * w_near + o_far[...].astype(jnp.float32) * w_far
    for h in range(cols // HEAD):
        out[:, h * HEAD : (h + 1) * HEAD] = whole[:, h * tok : (h + 1) * tok].T.astype(out.dtype)


VMEM = pl.BlockSpec(memory_space=pltpu.VMEM)
SMEM = pl.BlockSpec(memory_space=pltpu.SMEM)
PARAMS = dict(compiler_params=pltpu.CompilerParams(vmem_limit_bytes=48 * 1024 * 1024))


def local(queries, key_value_store, output_gradient, image_ids, image_counts, image_start):
    bf16, f32 = jnp.bfloat16, jnp.float32
    tok, cols = queries.shape
    width = tok * cols // HEAD
    n_tensor = lax.axis_size("tensor")
    n_dp = lax.axis_size("dp")
    me_t = lax.axis_index("tensor")
    me_d = lax.axis_index("dp")
    n_img, part_keys, store_cols = key_value_store.shape
    pair = store_cols // n_tensor
    keys = part_keys * n_tensor

    q_back = shift(queries, "dp", 1)
    g_back = shift(output_gradient, "dp", 1)

    pieces = []
    for k in range(n_tensor):
        piece = lax.dynamic_slice_in_dim(key_value_store, ((me_t + k) % n_tensor) * pair, pair, axis=2)
        pieces.append(piece if k == 0 else shift(piece, "tensor", k))
    kv = jnp.concatenate(pieces, axis=1)

    mine = me_d * IMG_DEV + jnp.arange(IMG_DEV, dtype=jnp.int32)
    rows = []
    for slot in range(2):
        sample = (me_d - slot) % n_dp
        ids, starts = image_ids[sample], image_start[sample]
        live = jnp.arange(ids.shape[0], dtype=jnp.int32) < image_counts[sample]
        hit = (ids[None, :] == mine[:, None]) & live[None, :]
        rows.append((jnp.any(hit, axis=1), jnp.sum(jnp.where(hit, starts[None, :], 0), axis=1)))
    slot_of = jnp.where(rows[0][0], 0, 1)
    start_of = jnp.where(rows[0][0], rows[0][1], rows[1][1])
    meta = jnp.stack([slot_of, start_of], axis=1).astype(jnp.int32)

    stat_shape = (2, 8, width)
    row_scratch = [pltpu.VMEM((2, width, HEAD), bf16), pltpu.VMEM((2, width, HEAD), bf16)]
    o_own, o_back, stats = pl.pallas_call(
        fwd_kernel,
        out_shape=(
            jax.ShapeDtypeStruct((HEAD, width), f32),
            jax.ShapeDtypeStruct((HEAD, width), bf16),
            jax.ShapeDtypeStruct(stat_shape, f32),
        ),
        in_specs=[SMEM] + [VMEM] * 5,
        out_specs=(VMEM, VMEM, VMEM),
        scratch_shapes=row_scratch + [
            pltpu.VMEM((keys, width), f32),
            pltpu.VMEM((8, 128), bf16),
            pltpu.VMEM((2, HEAD, width), f32),
        ],
        name="attend",
        **PARAMS,
    )(meta, queries, q_back, output_gradient, g_back, kv)

    far_own = shift(stats[1], "dp", -1)
    far_back = shift(stats[0], "dp", 1)
    o_far = shift(o_back, "dp", -1)

    dq_own, dq_back, dkv = pl.pallas_call(
        bwd_kernel,
        out_shape=(
            jax.ShapeDtypeStruct((tok, cols), f32),
            jax.ShapeDtypeStruct((tok, cols), bf16),
            jax.ShapeDtypeStruct((n_img, keys, pair), bf16),
        ),
        in_specs=[SMEM] + [VMEM] * 8,
        out_specs=(VMEM, VMEM, VMEM),
        scratch_shapes=row_scratch + [pltpu.VMEM((2, HEAD, width), f32)],
        name="backward",
        **PARAMS,
    )(meta, queries, q_back, output_gradient, g_back, kv, stats, far_own, far_back)

    dq_far = shift(dq_back, "dp", -1)
    returned = []
    for k in range(n_tensor):
        piece = dkv[:, k * part_keys : (k + 1) * part_keys, :]
        returned.append(piece if k == 0 else shift(piece, "tensor", -k))

    attended = pl.pallas_call(
        finish_kernel,
        out_shape=jax.ShapeDtypeStruct((tok, cols), bf16),
        in_specs=[VMEM] * 4,
        out_specs=VMEM,
        name="finish",
        **PARAMS,
    )(o_own, o_far, stats, far_own)
    grad_queries = (dq_own + dq_far.astype(f32)).astype(bf16)
    wide = jnp.stack(returned, axis=0)
    order = (jnp.arange(n_tensor) - me_t) % n_tensor
    grad_kv = jnp.concatenate(
        [lax.dynamic_index_in_dim(wide, order[h], 0, keepdims=False) for h in range(n_tensor)], axis=2
    )
    return attended, grad_queries, grad_kv


def solution(mesh):
    return jax.shard_map(
        local,
        mesh=mesh,
        in_specs=(P("dp", "tensor"), P("dp", "tensor", None), P("dp", "tensor"), P(), P(), P()),
        out_specs=(P("dp", "tensor"), P("dp", "tensor"), P("dp", "tensor", None)),
        check_vma=False,
    )
```

```python
import functools
import math

import jax
import jax.numpy as jnp
from jax import lax
from jax.experimental import pallas as pl
from jax.experimental.pallas import tpu as pltpu
from jax.sharding import PartitionSpec as P

HEAD = 128
IMG_DEV = 2
NEG_FILL = -1e30
BIG = 1e30
LOG2E = 1.4426950408889634
SCALE = HEAD ** (-0.5)
SCALE2 = SCALE * LOG2E

NT = (((1,), (1,)), ((), ()))
TN = (((0,), (0,)), ((), ()))
NN = (((1,), (0,)), ((), ()))


def dot(a, b, dims):
    return lax.dot_general(a, b, dims, preferred_element_type=jnp.float32)


def shift(value, axis, steps):
    count = lax.axis_size(axis)
    pairs = [(source, (source + steps) % count) for source in range(count)]
    return lax.ppermute(value, axis, pairs)


def stack_heads(src_ref, dst_ref, slot):
    rows, cols = src_ref.shape
    for h in range(cols // HEAD):
        dst_ref[slot, h * rows : (h + 1) * rows, :] = src_ref[:, h * HEAD : (h + 1) * HEAD]


def visible_rows(start, rows, width):
    pos = lax.broadcasted_iota(jnp.int32, (1, width), 1) % rows
    return pos >= start


def load_rows(refs, dst_ref):
    for slot, ref in enumerate(refs):
        stack_heads(ref, dst_ref, slot)


def split_kernel(axis, store, *pieces):
    n, width = len(pieces), pieces[0].shape[-1]
    for k, piece in enumerate(pieces):
        col = lax.rem(lax.axis_index(axis) + k, n) * width
        piece[...] = store[:, :, pl.ds(pl.multiple_of(col, width), width)]


def join_kernel(axis, *refs):
    pieces, out = refs[:-1], refs[-1]
    n, width = len(pieces), pieces[0].shape[-1]
    for k, piece in enumerate(pieces):
        col = lax.rem(lax.axis_index(axis) + k, n) * width
        out[:, :, pl.ds(pl.multiple_of(col, width), width)] = piece[...]


def fwd_kernel(first, last, blocks, *refs):
    refs = list(refs)
    meta, q_own, q_back = refs[:3]
    del refs[:3]
    if last:
        g_own, g_back = refs[:2]
        del refs[:2]
    kvs = refs[:blocks]
    del refs[:blocks]
    if not first:
        acc_in, stats_in = refs[:2]
        del refs[:2]
    if last:
        o_own, o_back, stats, qr, gr, acc = refs
    else:
        acc, stats, qr = refs
    tok, cols = q_own.shape
    width = tok * cols // HEAD
    load_rows((q_own, q_back), qr)
    if first:
        acc[...] = jnp.zeros_like(acc)
        stats[...] = jnp.zeros_like(stats)
        for slot in range(2):
            stats[slot, 0:1, :] = jnp.full((1, width), NEG_FILL, jnp.float32)
    else:
        acc[...] = acc_in[...]
        stats[...] = stats_in[...]
    for img in range(IMG_DEV):
        slot = meta[img, 0]
        seen = visible_rows(meta[img, 1], tok, width)
        scores = [dot(kv[img, :, :HEAD], qr[slot], NT) for kv in kvs]
        top = functools.reduce(jnp.maximum, [jnp.max(s, axis=0, keepdims=True) for s in scores])
        total = jnp.zeros((1, width), jnp.float32)
        out = jnp.zeros((HEAD, width), jnp.float32)
        for kv, s in zip(kvs, scores):
            part = jnp.exp2((s - top) * SCALE2)
            total = total + jnp.sum(part, axis=0, keepdims=True)
            out = out + dot(kv[img, :, HEAD:], part.astype(jnp.bfloat16), TN)
        old_top = stats[slot, 0:1, :]
        top = jnp.where(seen, top, NEG_FILL)
        new_top = jnp.maximum(old_top, top)
        old_w = jnp.exp2((old_top - new_top) * SCALE2)
        new_w = jnp.where(seen, jnp.exp2((top - new_top) * SCALE2), 0.0)
        stats[slot, 0:1, :] = new_top
        stats[slot, 1:2, :] = stats[slot, 1:2, :] * old_w + total * new_w
        acc[slot] = acc[slot] * old_w + out * new_w
    if last:
        load_rows((g_own, g_back), gr)
        eye = (
            lax.broadcasted_iota(jnp.int32, (HEAD, HEAD), 0)
            == lax.broadcasted_iota(jnp.int32, (HEAD, HEAD), 1)
        ).astype(jnp.bfloat16)
        for slot in range(2):
            total = stats[slot, 1:2, :]
            mean = acc[slot] * jnp.where(total > 0.0, 1.0 / jnp.maximum(total, 1e-30), 0.0)
            cot = dot(eye, gr[slot], NT)
            stats[slot, 2:3, :] = jnp.sum(cot * mean, axis=0, keepdims=True)
            if slot == 0:
                o_own[...] = mean
            else:
                o_back[...] = mean.astype(jnp.bfloat16)


def merge(first, second):
    top = jnp.maximum(first[0:1], second[0:1])
    w_first = first[1:2] * jnp.exp2((first[0:1] - top) * SCALE2)
    w_second = second[1:2] * jnp.exp2((second[0:1] - top) * SCALE2)
    total = w_first + w_second
    inv = jnp.where(total > 0.0, 1.0 / jnp.maximum(total, 1e-30), 0.0)
    return top, total, w_first * inv, w_second * inv


def bwd_kernel(first, last, blocks, *refs):
    refs = list(refs)
    meta, q_own, q_back, g_own, g_back, stats, far_own, far_back = refs[:8]
    del refs[:8]
    kvs = refs[:blocks]
    del refs[:blocks]
    if not first:
        acc_in = refs.pop(0)
    if last:
        dq_own, dq_back = refs[:2]
        del refs[:2]
    else:
        acc = refs.pop(0)
    dkvs = refs[:blocks]
    del refs[:blocks]
    if last:
        qr, gr, acc = refs
    else:
        qr, gr = refs
    tok, cols = q_own.shape
    width = tok * cols // HEAD
    load_rows((q_own, q_back), qr)
    load_rows((g_own, g_back), gr)
    acc[...] = jnp.zeros_like(acc) if first else acc_in[...]
    logs, deltas = [], []
    for slot, far in ((0, far_own), (1, far_back)):
        near_v = stats[slot]
        far_v = far[...]
        top, total, w_near, w_far = merge(near_v, far_v)
        logs.append(jnp.where(total > 0.0, top * SCALE2 + jnp.log(jnp.maximum(total, 1e-30)) * LOG2E, 0.0))
        deltas.append(w_near * near_v[2:3] + w_far * far_v[2:3])
    for img in range(IMG_DEV):
        slot = meta[img, 0]
        seen = visible_rows(meta[img, 1], tok, width)
        log_total = jnp.where(slot == 0, logs[0], logs[1])
        log_total = jnp.where(seen, log_total, BIG)
        delta = jnp.where(slot == 0, deltas[0], deltas[1])
        for kv, dkv in zip(kvs, dkvs):
            key = kv[img, :, :HEAD]
            part = jnp.exp2(dot(key, qr[slot], NT) * SCALE2 - log_total)
            dweight = dot(kv[img, :, HEAD:], gr[slot], NT)
            ds = (part * (dweight - delta)).astype(jnp.bfloat16)
            dkv[img, :, HEAD:] = dot(part.astype(jnp.bfloat16), gr[slot], NN).astype(jnp.bfloat16)
            dkv[img, :, :HEAD] = (dot(ds, qr[slot], NN) * SCALE).astype(jnp.bfloat16)
            acc[slot] = acc[slot] + dot(key, ds, TN)
    if last:
        for slot, out in ((0, dq_own), (1, dq_back)):
            for h in range(cols // HEAD):
                block = acc[slot, :, h * tok : (h + 1) * tok] * SCALE
                out[:, h * HEAD : (h + 1) * HEAD] = block.T.astype(out.dtype)


def finish_kernel(o_own, o_far, stats, far, dq_own, dq_far, out, dq):
    tok, cols = out.shape
    _, _, w_near, w_far = merge(stats[0], far[...])
    whole = o_own[...] * w_near + o_far[...].astype(jnp.float32) * w_far
    for h in range(cols // HEAD):
        out[:, h * HEAD : (h + 1) * HEAD] = whole[:, h * tok : (h + 1) * tok].T.astype(out.dtype)
    dq[...] = (dq_own[...] + dq_far[...].astype(jnp.float32)).astype(dq.dtype)


VMEM = pl.BlockSpec(memory_space=pltpu.VMEM)
SMEM = pl.BlockSpec(memory_space=pltpu.SMEM)


def call(kernel, name, outs, operands, scratch=(), smem=0, flops=0):
    return pl.pallas_call(
        kernel,
        out_shape=[jax.ShapeDtypeStruct(*o) for o in outs],
        in_specs=[SMEM] * smem + [VMEM] * (len(operands) - smem),
        out_specs=[VMEM] * len(outs),
        scratch_shapes=list(scratch),
        compiler_params=pltpu.CompilerParams(vmem_limit_bytes=32 * 1024 * 1024),
        cost_estimate=pl.CostEstimate(flops=flops, bytes_accessed=1 << 20, transcendentals=0),
        name=name,
    )(*operands)


def hop(value, steps):
    count = lax.axis_size("dp")
    half = count // 2
    pairs = [(s, (s + steps) % count) for s in range(count) if s // half == (s + steps) % count // half]
    return lax.ppermute(value, "dp", pairs)


def over_seam(value, steps):
    count = lax.axis_size("dp")
    half = count // 2
    groups = [list(range(half)), list(range(half, count))]
    source = half - 1 if steps > 0 else 0
    spread = lax.all_to_all(value, "dp", 0, 0, axis_index_groups=groups, tiled=True)
    rows = value.shape[0] // half
    part = spread[source * rows : (source + 1) * rows]
    part = lax.ppermute(part, "dp", [(s, (s + half) % count) for s in range(count)])
    return lax.all_gather(part, "dp", axis_index_groups=groups, tiled=True)


def local(queries, key_value_store, output_gradient, image_ids, image_counts, image_start):
    bf16, f32 = jnp.bfloat16, jnp.float32
    tok, cols = queries.shape
    width = tok * cols // HEAD
    n = lax.axis_size("tensor")
    n_dp = lax.axis_size("dp")
    me_d = lax.axis_index("dp")
    n_img, part_keys, store_cols = key_value_store.shape
    pair = store_cols // n
    piece_shape = ((n_img, part_keys, pair), bf16)
    after = lambda value, *others: lax.optimization_barrier((value, *others))[0]
    block_flops = n_img * part_keys * width * HEAD * 2

    sends = call(functools.partial(split_kernel, "tensor"), "split", [piece_shape] * n, (key_value_store,))
    half = n // 2
    waves = [[half], [half - 1, half + 1], [k for d in range(half - 2, 0, -1) for k in (d, n - d)]]
    kv = {0: sends[0]}
    for i, wave in enumerate(waves):
        for k in wave:
            kv[k] = shift(after(sends[k], kv[half]) if i == 2 else sends[k], "tensor", k)

    both = after(jnp.concatenate([queries, output_gradient], axis=0), kv[half])
    on_seam = me_d % (n_dp // 2) == 0
    both_back = jnp.where(on_seam, over_seam(both, 1), hop(both, 1))
    q_back, g_back = both_back[:tok], both_back[tok:]

    mine = me_d * IMG_DEV + jnp.arange(IMG_DEV, dtype=jnp.int32)
    rows = []
    for slot in range(2):
        sample = (me_d - slot) % n_dp
        ids, starts = image_ids[sample], image_start[sample]
        live = jnp.arange(ids.shape[0], dtype=jnp.int32) < image_counts[sample]
        hit = (ids[None, :] == mine[:, None]) & live[None, :]
        rows.append((jnp.any(hit, axis=1), jnp.sum(jnp.where(hit, starts[None, :], 0), axis=1)))
    slot_of = jnp.where(rows[0][0], 0, 1)
    start_of = jnp.where(rows[0][0], rows[0][1], rows[1][1])
    meta = jnp.stack([slot_of, start_of], axis=1).astype(jnp.int32)

    stat_shape = ((2, 8, width), f32)
    acc_shape = ((2, HEAD, width), f32)
    rows_scratch = pltpu.VMEM((2, width, HEAD), bf16)
    state = ()
    stages = [[0] + waves[0] + waves[1], waves[2][:-2], waves[2][-2:]]
    for i, stage in enumerate(stages):
        first, last = i == 0, i == len(stages) - 1
        operands = (meta, queries, q_back) + ((output_gradient, g_back) if last else ())
        operands += tuple(kv[k] for k in stage) + tuple(state)
        outs = [((HEAD, width), f32), ((HEAD, width), bf16), stat_shape] if last else [acc_shape, stat_shape]
        scratch = [rows_scratch] + ([rows_scratch, pltpu.VMEM(*acc_shape)] if last else [])
        state = call(
            functools.partial(fwd_kernel, first, last, len(stage)), "attend", outs, operands, scratch, 1,
            2 * len(stage) * block_flops,
        )
    o_own, o_back, stats = state

    far_own = shift(stats[1], "dp", -1)
    far_back = shift(stats[0], "dp", 1)

    back = {}
    acc = ()
    parts = [waves[0] + waves[1], waves[2] + [0]]
    for i, stage in enumerate(parts):
        first, last = i == 0, i == len(parts) - 1
        operands = (meta, queries, q_back, output_gradient, g_back, stats, far_own, far_back)
        if not first:
            acc = (after(acc[0], back[half]),)
        operands += tuple(kv[k] for k in stage) + tuple(acc)
        outs = [((tok, cols), f32), ((tok, cols), bf16)] if last else [acc_shape]
        scratch = [rows_scratch] * 2 + ([pltpu.VMEM(*acc_shape)] if last else [])
        got = call(
            functools.partial(bwd_kernel, first, last, len(stage)), "backward", outs + [piece_shape] * len(stage),
            operands, scratch, 1, 5 * len(stage) * block_flops,
        )
        for k, piece in zip(stage, got[len(outs) :]):
            back[k] = shift(piece, "tensor", -k) if k else piece
        acc = got[: len(outs)]
    dq_own, dq_back = acc

    both = jnp.concatenate([o_back.reshape(tok, cols), dq_back], axis=0)
    on_seam = me_d % (n_dp // 2) == n_dp // 2 - 1
    both_far = jnp.where(on_seam, over_seam(both, -1), hop(both, -1))
    o_far, dq_far = both_far[:tok].reshape(HEAD, width), both_far[tok:]

    attended, grad_queries = call(
        finish_kernel, "finish", [((tok, cols), bf16)] * 2, (o_own, o_far, stats, far_own, dq_own, dq_far)
    )
    (grad_kv,) = call(
        functools.partial(join_kernel, "tensor"), "join", [((n_img, part_keys, store_cols), bf16)],
        [after(back[0], attended)] + [back[k] for k in range(1, n)],
    )
    return attended, grad_queries, grad_kv


def solution(mesh):
    return jax.shard_map(
        local,
        mesh=mesh,
        in_specs=(P("dp", "tensor"), P("dp", "tensor", None), P("dp", "tensor"), P(), P(), P()),
        out_specs=(P("dp", "tensor"), P("dp", "tensor"), P("dp", "tensor", None)),
        check_vma=False,
    )
```

```python
import functools
import math

import jax
import jax.numpy as jnp
from jax import lax
from jax.experimental import pallas as pl
from jax.experimental.pallas import tpu as pltpu
from jax.sharding import PartitionSpec as P

HEAD = 128
IMG_DEV = 2
NEG_FILL = -1e30
BIG = 1e30
LOG2E = 1.4426950408889634
SCALE = HEAD ** (-0.5)
SCALE2 = SCALE * LOG2E
WINDOW = 4

NT = (((1,), (1,)), ((), ()))
TN = (((0,), (0,)), ((), ()))
NN = (((1,), (0,)), ((), ()))


def dot(a, b, dims):
    return lax.dot_general(a, b, dims, preferred_element_type=jnp.float32)


def shift(value, axis, steps):
    count = lax.axis_size(axis)
    pairs = [(source, (source + steps) % count) for source in range(count)]
    return lax.ppermute(value, axis, pairs)


def stack_heads(src_ref, dst_ref, slot):
    rows, cols = src_ref.shape
    for h in range(cols // HEAD):
        dst_ref[slot, h * rows : (h + 1) * rows, :] = src_ref[:, h * HEAD : (h + 1) * HEAD]


def visible_rows(start, rows, width):
    pos = lax.broadcasted_iota(jnp.int32, (1, width), 1) % rows
    return pos >= start


def load_rows(refs, dst_ref):
    for slot, ref in enumerate(refs):
        stack_heads(ref, dst_ref, slot)


def split_kernel(axis, store, *pieces):
    n, width = len(pieces), pieces[0].shape[-1]
    for k, piece in enumerate(pieces):
        col = lax.rem(lax.axis_index(axis) + k, n) * width
        piece[...] = store[:, :, pl.ds(pl.multiple_of(col, width), width)]


def join_kernel(axis, shifts, *refs):
    pieces, out = refs[-1 - len(shifts) : -1], refs[-1]
    width = pieces[0].shape[-1]
    n = out.shape[-1] // width
    for k, piece in zip(shifts, pieces):
        col = lax.rem(lax.axis_index(axis) + k, n) * width
        out[:, :, pl.ds(pl.multiple_of(col, width), width)] = piece[...]


def fwd_kernel(first, last, blocks, *refs):
    refs = list(refs)
    meta, q_own, q_back = refs[:3]
    del refs[:3]
    if last:
        g_own, g_back = refs[:2]
        del refs[:2]
    kvs = refs[:blocks]
    del refs[:blocks]
    if not first:
        acc_in, stats_in = refs[:2]
        del refs[:2]
    if last:
        o_own, o_back, stats, qr, gr, acc = refs
    else:
        acc, stats, qr = refs
    tok, cols = q_own.shape
    width = tok * cols // HEAD
    load_rows((q_own, q_back), qr)
    if first:
        acc[...] = jnp.zeros_like(acc)
        stats[...] = jnp.zeros_like(stats)
        for slot in range(2):
            stats[slot, 0:1, :] = jnp.full((1, width), NEG_FILL, jnp.float32)
    else:
        acc[...] = acc_in[...]
        stats[...] = stats_in[...]
    for img in range(IMG_DEV):
        slot = meta[img, 0]
        seen = visible_rows(meta[img, 1], tok, width)
        scores = [dot(kv[img, :, :HEAD], qr[slot], NT) for kv in kvs]
        top = functools.reduce(jnp.maximum, [jnp.max(s, axis=0, keepdims=True) for s in scores])
        total = jnp.zeros((1, width), jnp.float32)
        out = jnp.zeros((HEAD, width), jnp.float32)
        for kv, s in zip(kvs, scores):
            part = jnp.exp2((s - top) * SCALE2)
            total = total + jnp.sum(part, axis=0, keepdims=True)
            out = out + dot(kv[img, :, HEAD:], part.astype(jnp.bfloat16), TN)
        old_top = stats[slot, 0:1, :]
        top = jnp.where(seen, top, NEG_FILL)
        new_top = jnp.maximum(old_top, top)
        old_w = jnp.exp2((old_top - new_top) * SCALE2)
        new_w = jnp.where(seen, jnp.exp2((top - new_top) * SCALE2), 0.0)
        stats[slot, 0:1, :] = new_top
        stats[slot, 1:2, :] = stats[slot, 1:2, :] * old_w + total * new_w
        acc[slot] = acc[slot] * old_w + out * new_w
    if last:
        load_rows((g_own, g_back), gr)
        eye = (
            lax.broadcasted_iota(jnp.int32, (HEAD, HEAD), 0)
            == lax.broadcasted_iota(jnp.int32, (HEAD, HEAD), 1)
        ).astype(jnp.bfloat16)
        for slot in range(2):
            total = stats[slot, 1:2, :]
            mean = acc[slot] * jnp.where(total > 0.0, 1.0 / jnp.maximum(total, 1e-30), 0.0)
            cot = dot(eye, gr[slot], NT)
            stats[slot, 2:3, :] = jnp.sum(cot * mean, axis=0, keepdims=True)
            if slot == 0:
                o_own[...] = mean
            else:
                o_back[...] = mean.astype(jnp.bfloat16)


def merge(first, second):
    top = jnp.maximum(first[0:1], second[0:1])
    w_first = first[1:2] * jnp.exp2((first[0:1] - top) * SCALE2)
    w_second = second[1:2] * jnp.exp2((second[0:1] - top) * SCALE2)
    total = w_first + w_second
    inv = jnp.where(total > 0.0, 1.0 / jnp.maximum(total, 1e-30), 0.0)
    return top, total, w_first * inv, w_second * inv


def bwd_kernel(first, last, blocks, *refs):
    refs = list(refs)
    meta, q_own, q_back, g_own, g_back, stats, far_own, far_back = refs[:8]
    del refs[:8]
    kvs = refs[:blocks]
    del refs[:blocks]
    if not first:
        acc_in = refs.pop(0)
    if last:
        dq_own, dq_back = refs[:2]
        del refs[:2]
    else:
        acc = refs.pop(0)
    dkvs = refs[:blocks]
    del refs[:blocks]
    if last:
        qr, gr, acc = refs
    else:
        qr, gr = refs
    tok, cols = q_own.shape
    width = tok * cols // HEAD
    load_rows((q_own, q_back), qr)
    load_rows((g_own, g_back), gr)
    acc[...] = jnp.zeros_like(acc) if first else acc_in[...]
    logs, deltas = [], []
    for slot, far in ((0, far_own), (1, far_back)):
        near_v = stats[slot]
        far_v = far[...]
        top, total, w_near, w_far = merge(near_v, far_v)
        logs.append(jnp.where(total > 0.0, top * SCALE2 + jnp.log(jnp.maximum(total, 1e-30)) * LOG2E, 0.0))
        deltas.append(w_near * near_v[2:3] + w_far * far_v[2:3])
    for img in range(IMG_DEV):
        slot = meta[img, 0]
        seen = visible_rows(meta[img, 1], tok, width)
        log_total = jnp.where(slot == 0, logs[0], logs[1])
        log_total = jnp.where(seen, log_total, BIG)
        delta = jnp.where(slot == 0, deltas[0], deltas[1])
        for kv, dkv in zip(kvs, dkvs):
            key = kv[img, :, :HEAD]
            part = jnp.exp2(dot(key, qr[slot], NT) * SCALE2 - log_total)
            dweight = dot(kv[img, :, HEAD:], gr[slot], NT)
            ds = (part * (dweight - delta)).astype(jnp.bfloat16)
            dkv[img, :, HEAD:] = dot(part.astype(jnp.bfloat16), gr[slot], NN).astype(jnp.bfloat16)
            dkv[img, :, :HEAD] = (dot(ds, qr[slot], NN) * SCALE).astype(jnp.bfloat16)
            acc[slot] = acc[slot] + dot(key, ds, TN)
    if last:
        for slot, out in ((0, dq_own), (1, dq_back)):
            for h in range(cols // HEAD):
                block = acc[slot, :, h * tok : (h + 1) * tok] * SCALE
                out[:, h * HEAD : (h + 1) * HEAD] = block.T.astype(out.dtype)


def finish_kernel(o_own, o_far, stats, far, dq_own, dq_far, out, dq):
    tok, cols = out.shape
    _, _, w_near, w_far = merge(stats[0], far[...])
    whole = o_own[...] * w_near + o_far[...].astype(jnp.float32) * w_far
    for h in range(cols // HEAD):
        out[:, h * HEAD : (h + 1) * HEAD] = whole[:, h * tok : (h + 1) * tok].T.astype(out.dtype)
    dq[...] = (dq_own[...] + dq_far[...].astype(jnp.float32)).astype(dq.dtype)


VMEM = pl.BlockSpec(memory_space=pltpu.VMEM)
SMEM = pl.BlockSpec(memory_space=pltpu.SMEM)


def call(kernel, name, outs, operands, scratch=(), smem=0, flops=0, aliases=None):
    return pl.pallas_call(
        kernel,
        out_shape=[jax.ShapeDtypeStruct(*o) for o in outs],
        in_specs=[SMEM] * smem + [VMEM] * (len(operands) - smem),
        out_specs=[VMEM] * len(outs),
        scratch_shapes=list(scratch),
        compiler_params=pltpu.CompilerParams(vmem_limit_bytes=32 * 1024 * 1024),
        cost_estimate=pl.CostEstimate(flops=flops, bytes_accessed=1 << 20, transcendentals=0),
        input_output_aliases=aliases or {},
        name=name,
    )(*operands)


def after(value, *others):
    return lax.optimization_barrier((value, *others))[0]


def within(value, steps):
    count = lax.axis_size("dp")
    half = count // 2
    inside = [(s, s + steps) for s in range(count) if s // half == (s + steps) // half and s + steps >= 0]
    return lax.ppermute(value, "dp", inside)


def seam_legs(steps):
    count, n = lax.axis_size("dp"), lax.axis_size("tensor")
    half = count // 2
    source, near = (half - 1, 0) if steps > 0 else (0, half - 1)
    relays = [31, 0, 25, 7, 29, 23, 3, 9] if half == 32 and n == 8 else [half - 1] * n

    def send(part, pairs):
        return lax.ppermute(part, ("dp", "tensor"), [(d * n + t, e * n + t) for d, e, t in pairs])

    fan = [(source + base, relays[t] + base, t) for base in (0, half) for t in range(n)]
    over = [(relays[t] + base, near + half - base, t) for base in (0, half) for t in range(n)]
    return lambda part: send(part, fan), lambda part: send(part, over)


def exchange(pieces, order, sign, both, steps):
    half = lax.axis_size("dp") // 2
    near = 0 if steps > 0 else half - 1
    first_leg, second_leg = seam_legs(steps)
    fan = first_leg(both)
    got = {}
    for i, k in enumerate(order):
        gate = fan if i < WINDOW else got[order[i - WINDOW]]
        got[k] = shift(after(pieces[k], gate), "tensor", sign * k) if k else pieces[k]
    both = jnp.where(lax.axis_index("dp") % half == near, second_leg(fan), within(both, steps))
    return got, both


def local(queries, key_value_store, output_gradient, image_ids, image_counts, image_start):
    bf16, f32 = jnp.bfloat16, jnp.float32
    tok, cols = queries.shape
    width = tok * cols // HEAD
    n = lax.axis_size("tensor")
    n_dp = lax.axis_size("dp")
    me_d = lax.axis_index("dp")
    n_img, part_keys, store_cols = key_value_store.shape
    pair = store_cols // n
    piece_shape = ((n_img, part_keys, pair), bf16)

    sends = call(functools.partial(split_kernel, "tensor"), "split", [piece_shape] * n, (key_value_store,))
    order = [k for d in range(n // 2, 0, -1) for k in sorted({d, n - d})] + [0]
    both = jnp.concatenate([queries, output_gradient], axis=0)
    kv, both = exchange(sends, order, 1, both, 1)
    q_back, g_back = both[:tok], both[tok:]

    mine = me_d * IMG_DEV + jnp.arange(IMG_DEV, dtype=jnp.int32)
    rows = []
    for slot in range(2):
        sample = (me_d - slot) % n_dp
        ids, starts = image_ids[sample], image_start[sample]
        live = jnp.arange(ids.shape[0], dtype=jnp.int32) < image_counts[sample]
        hit = (ids[None, :] == mine[:, None]) & live[None, :]
        rows.append((jnp.any(hit, axis=1), jnp.sum(jnp.where(hit, starts[None, :], 0), axis=1)))
    slot_of = jnp.where(rows[0][0], 0, 1)
    start_of = jnp.where(rows[0][0], rows[0][1], rows[1][1])
    meta = jnp.stack([slot_of, start_of], axis=1).astype(jnp.int32)

    stat_shape = ((2, 8, width), f32)
    acc_shape = ((2, HEAD, width), f32)
    rows_scratch = pltpu.VMEM((2, width, HEAD), bf16)
    o_own, o_back, stats = call(
        functools.partial(fwd_kernel, True, True, n), "attend",
        [((HEAD, width), f32), ((HEAD, width), bf16), stat_shape],
        (meta, queries, q_back, output_gradient, g_back) + tuple(kv[k] for k in order),
        [rows_scratch, rows_scratch, pltpu.VMEM(*acc_shape)], 1,
    )

    far_own = shift(stats[1], "dp", -1)
    far_back = shift(stats[0], "dp", 1)

    operands = (meta, queries, q_back, output_gradient, g_back, stats, far_own, far_back)
    dq_own, dq_back, *pieces = call(
        functools.partial(bwd_kernel, True, True, n), "backward",
        [((tok, cols), f32), ((tok, cols), bf16)] + [piece_shape] * n,
        operands + tuple(kv[k] for k in order), [rows_scratch] * 2 + [pltpu.VMEM(*acc_shape)], 1,
    )
    both = jnp.concatenate([o_back.reshape(tok, cols), dq_back], axis=0)
    back, both = exchange(dict(zip(order, pieces)), order, -1, both, -1)
    o_far, dq_far = both[:tok].reshape(HEAD, width), both[tok:]

    attended, grad_queries = call(
        finish_kernel, "finish", [((tok, cols), bf16)] * 2, (o_own, o_far, stats, far_own, dq_own, dq_far)
    )
    (grad_kv,) = call(
        functools.partial(join_kernel, "tensor", range(n)), "join", [((n_img, part_keys, store_cols), bf16)],
        [back[k] for k in range(n)],
    )
    return attended, grad_queries, grad_kv


def solution(mesh):
    return jax.shard_map(
        local,
        mesh=mesh,
        in_specs=(P("dp", "tensor"), P("dp", "tensor", None), P("dp", "tensor"), P(), P(), P()),
        out_specs=(P("dp", "tensor"), P("dp", "tensor"), P("dp", "tensor", None)),
        check_vma=False,
    )
```

```python
import functools
import math

import jax
import jax.numpy as jnp
from jax import lax
from jax.experimental import pallas as pl
from jax.experimental.pallas import tpu as pltpu
from jax.sharding import PartitionSpec as P

HEAD = 128
IMG_DEV = 2
NEG_FILL = -1e30
BIG = 1e30
LOG2E = 1.4426950408889634
SCALE = HEAD ** (-0.5)
SCALE2 = SCALE * LOG2E
WINDOW = 4

NT = (((1,), (1,)), ((), ()))
TN = (((0,), (0,)), ((), ()))
NN = (((1,), (0,)), ((), ()))


def dot(a, b, dims):
    return lax.dot_general(a, b, dims, preferred_element_type=jnp.float32)


def shift(value, axis, steps):
    count = lax.axis_size(axis)
    pairs = [(source, (source + steps) % count) for source in range(count)]
    return lax.ppermute(value, axis, pairs)


def stack_heads(src_ref, dst_ref, slot):
    rows, cols = src_ref.shape
    for h in range(cols // HEAD):
        dst_ref[slot, h * rows : (h + 1) * rows, :] = src_ref[:, h * HEAD : (h + 1) * HEAD]


def visible_rows(start, rows, width):
    pos = lax.broadcasted_iota(jnp.int32, (1, width), 1) % rows
    return pos >= start


def load_rows(refs, dst_ref):
    for slot, ref in enumerate(refs):
        stack_heads(ref, dst_ref, slot)


def split_kernel(axis, queries, cots, store, both, *pieces):
    n, width = len(pieces), pieces[0].shape[-1]
    tok = queries.shape[0]
    both[:tok, :] = queries[...]
    both[tok:, :] = cots[...]
    for k, piece in enumerate(pieces):
        col = lax.rem(lax.axis_index(axis) + k, n) * width
        piece[...] = store[:, :, pl.ds(pl.multiple_of(col, width), width)]


def fwd_kernel(first, last, blocks, *refs):
    refs = list(refs)
    meta, q_own, q_back = refs[:3]
    del refs[:3]
    if last:
        g_own, g_back = refs[:2]
        del refs[:2]
    kvs = refs[:blocks]
    del refs[:blocks]
    if not first:
        acc_in, stats_in = refs[:2]
        del refs[:2]
    if last:
        o_own, o_back, stats, qr, gr, acc = refs
    else:
        acc, stats, qr = refs
    tok, cols = q_own.shape
    width = tok * cols // HEAD
    load_rows((q_own, q_back), qr)
    if first:
        acc[...] = jnp.zeros_like(acc)
        stats[...] = jnp.zeros_like(stats)
        for slot in range(2):
            stats[slot, 0:1, :] = jnp.full((1, width), NEG_FILL, jnp.float32)
    else:
        acc[...] = acc_in[...]
        stats[...] = stats_in[...]
    for img in range(IMG_DEV):
        slot = meta[img, 0]
        seen = visible_rows(meta[img, 1], tok, width)
        scores = [dot(kv[img, :, :HEAD], qr[slot], NT) for kv in kvs]
        top = functools.reduce(jnp.maximum, [jnp.max(s, axis=0, keepdims=True) for s in scores])
        total = jnp.zeros((1, width), jnp.float32)
        out = jnp.zeros((HEAD, width), jnp.float32)
        for kv, s in zip(kvs, scores):
            part = jnp.exp2((s - top) * SCALE2)
            total = total + jnp.sum(part, axis=0, keepdims=True)
            out = out + dot(kv[img, :, HEAD:], part.astype(jnp.bfloat16), TN)
        old_top = stats[slot, 0:1, :]
        top = jnp.where(seen, top, NEG_FILL)
        new_top = jnp.maximum(old_top, top)
        old_w = jnp.exp2((old_top - new_top) * SCALE2)
        new_w = jnp.where(seen, jnp.exp2((top - new_top) * SCALE2), 0.0)
        stats[slot, 0:1, :] = new_top
        stats[slot, 1:2, :] = stats[slot, 1:2, :] * old_w + total * new_w
        acc[slot] = acc[slot] * old_w + out * new_w
    if last:
        load_rows((g_own, g_back), gr)
        eye = (
            lax.broadcasted_iota(jnp.int32, (HEAD, HEAD), 0)
            == lax.broadcasted_iota(jnp.int32, (HEAD, HEAD), 1)
        ).astype(jnp.bfloat16)
        for slot in range(2):
            total = stats[slot, 1:2, :]
            mean = acc[slot] * jnp.where(total > 0.0, 1.0 / jnp.maximum(total, 1e-30), 0.0)
            cot = dot(eye, gr[slot], NT)
            stats[slot, 2:3, :] = jnp.sum(cot * mean, axis=0, keepdims=True)
            if slot == 0:
                o_own[...] = mean
            else:
                o_back[...] = mean.astype(jnp.bfloat16)


def merge(first, second):
    top = jnp.maximum(first[0:1], second[0:1])
    w_first = first[1:2] * jnp.exp2((first[0:1] - top) * SCALE2)
    w_second = second[1:2] * jnp.exp2((second[0:1] - top) * SCALE2)
    total = w_first + w_second
    inv = jnp.where(total > 0.0, 1.0 / jnp.maximum(total, 1e-30), 0.0)
    return top, total, w_first * inv, w_second * inv


def bwd_kernel(first, last, blocks, *refs):
    refs = list(refs)
    meta, q_own, q_back, g_own, g_back, stats, far_own, far_back = refs[:8]
    del refs[:8]
    kvs = refs[:blocks]
    del refs[:blocks]
    if not first:
        acc_in = refs.pop(0)
    if last:
        dq_own, dq_back = refs[:2]
        del refs[:2]
    else:
        acc = refs.pop(0)
    dkvs = refs[:blocks]
    del refs[:blocks]
    if last:
        qr, gr, acc = refs
    else:
        qr, gr = refs
    tok, cols = q_own.shape
    width = tok * cols // HEAD
    load_rows((q_own, q_back), qr)
    load_rows((g_own, g_back), gr)
    acc[...] = jnp.zeros_like(acc) if first else acc_in[...]
    logs, deltas = [], []
    for slot, far in ((0, far_own), (1, far_back)):
        near_v = stats[slot]
        far_v = far[...]
        top, total, w_near, w_far = merge(near_v, far_v)
        logs.append(jnp.where(total > 0.0, top * SCALE2 + jnp.log(jnp.maximum(total, 1e-30)) * LOG2E, 0.0))
        deltas.append(w_near * near_v[2:3] + w_far * far_v[2:3])
    for img in range(IMG_DEV):
        slot = meta[img, 0]
        seen = visible_rows(meta[img, 1], tok, width)
        log_total = jnp.where(slot == 0, logs[0], logs[1])
        log_total = jnp.where(seen, log_total, BIG)
        delta = jnp.where(slot == 0, deltas[0], deltas[1])
        for kv, dkv in zip(kvs, dkvs):
            key = kv[img, :, :HEAD]
            part = jnp.exp2(dot(key, qr[slot], NT) * SCALE2 - log_total)
            dweight = dot(kv[img, :, HEAD:], gr[slot], NT)
            ds = (part * (dweight - delta)).astype(jnp.bfloat16)
            dkv[img, :, HEAD:] = dot(part.astype(jnp.bfloat16), gr[slot], NN).astype(jnp.bfloat16)
            dkv[img, :, :HEAD] = (dot(ds, qr[slot], NN) * SCALE).astype(jnp.bfloat16)
            acc[slot] = acc[slot] + dot(key, ds, TN)
    if last:
        for slot, out in ((0, dq_own), (1, dq_back)):
            for h in range(cols // HEAD):
                block = acc[slot, :, h * tok : (h + 1) * tok] * SCALE
                out[:, h * HEAD : (h + 1) * HEAD] = block.T.astype(out.dtype)


def finish_kernel(axis, o_own, stats, far, dq_own, both, *refs):
    pieces, (out, dq, dkv) = refs[:-3], refs[-3:]
    tok, cols = out.shape
    n, pair = len(pieces), pieces[0].shape[-1]
    for k, piece in enumerate(pieces):
        col = lax.rem(lax.axis_index(axis) + k, n) * pair
        dkv[:, :, pl.ds(pl.multiple_of(col, pair), pair)] = piece[...]
    _, _, w_near, w_far = merge(stats[0], far[...])
    for h in range(cols // HEAD):
        rows = slice(h * tok, (h + 1) * tok)
        whole = o_own[:, rows] * w_near[:, rows] + both[:tok, rows].astype(jnp.float32) * w_far[:, rows]
        out[:, h * HEAD : (h + 1) * HEAD] = whole.T.astype(out.dtype)
    dq[...] = (dq_own[...] + both[tok:, :].astype(jnp.float32)).astype(dq.dtype)


VMEM = pl.BlockSpec(memory_space=pltpu.VMEM)
SMEM = pl.BlockSpec(memory_space=pltpu.SMEM)


def call(kernel, name, outs, operands, scratch=(), smem=0, flops=0, aliases=None):
    return pl.pallas_call(
        kernel,
        out_shape=[jax.ShapeDtypeStruct(*o) for o in outs],
        in_specs=[SMEM] * smem + [VMEM] * (len(operands) - smem),
        out_specs=[VMEM] * len(outs),
        scratch_shapes=list(scratch),
        compiler_params=pltpu.CompilerParams(vmem_limit_bytes=32 * 1024 * 1024),
        cost_estimate=pl.CostEstimate(flops=flops, bytes_accessed=1 << 20, transcendentals=0),
        input_output_aliases=aliases or {},
        name=name,
    )(*operands)


def after(value, *others):
    return lax.optimization_barrier((value, *others))[0]


def within(value, steps):
    count = lax.axis_size("dp")
    half = count // 2
    inside = [(s, s + steps) for s in range(count) if s // half == (s + steps) // half and s + steps >= 0]
    return lax.ppermute(value, "dp", inside)


def seam_legs(steps):
    count, n = lax.axis_size("dp"), lax.axis_size("tensor")
    half = count // 2
    source, near = (half - 1, 0) if steps > 0 else (0, half - 1)
    relays = [5, 17, 25, 7, 29, 23, 3, 9] if half == 32 and n == 8 else [half - 1] * n

    def send(part, pairs):
        return lax.ppermute(part, ("dp", "tensor"), [(d * n + t, e * n + t) for d, e, t in pairs])

    fan = [(source + base, relays[t] + base, t) for base in (0, half) for t in range(n)]
    over = [(relays[t] + base, near + half - base, t) for base in (0, half) for t in range(n)]
    return lambda part: send(part, fan), lambda part: send(part, over)


def exchange(pieces, order, sign, both, steps):
    half = lax.axis_size("dp") // 2
    near = 0 if steps > 0 else half - 1
    first_leg, second_leg = seam_legs(steps)
    got = {}
    for i, k in enumerate(order):
        piece = after(pieces[k], got[order[i - WINDOW]]) if i >= WINDOW else pieces[k]
        got[k] = shift(piece, "tensor", sign * k) if k else piece
    over = second_leg(first_leg(both))
    both = jnp.where(lax.axis_index("dp") % half == near, over, within(both, steps))
    return got, both


def local(queries, key_value_store, output_gradient, image_ids, image_counts, image_start):
    bf16, f32 = jnp.bfloat16, jnp.float32
    tok, cols = queries.shape
    width = tok * cols // HEAD
    n = lax.axis_size("tensor")
    n_dp = lax.axis_size("dp")
    me_d = lax.axis_index("dp")
    n_img, part_keys, store_cols = key_value_store.shape
    pair = store_cols // n
    piece_shape = ((n_img, part_keys, pair), bf16)

    both, *sends = call(
        functools.partial(split_kernel, "tensor"), "split", [((2 * tok, cols), bf16)] + [piece_shape] * n,
        (queries, output_gradient, key_value_store),
    )
    order = [1, n - 1, n // 2] + [k for d in range(2, n // 2) for k in (d, n - d)] + [0]
    kv, both = exchange(sends, order, 1, both, 1)
    q_back, g_back = both[:tok], both[tok:]

    mine = me_d * IMG_DEV + jnp.arange(IMG_DEV, dtype=jnp.int32)
    rows = []
    for slot in range(2):
        sample = (me_d - slot) % n_dp
        ids, starts = image_ids[sample], image_start[sample]
        live = jnp.arange(ids.shape[0], dtype=jnp.int32) < image_counts[sample]
        hit = (ids[None, :] == mine[:, None]) & live[None, :]
        rows.append((jnp.any(hit, axis=1), jnp.sum(jnp.where(hit, starts[None, :], 0), axis=1)))
    slot_of = jnp.where(rows[0][0], 0, 1)
    start_of = jnp.where(rows[0][0], rows[0][1], rows[1][1])
    meta = jnp.stack([slot_of, start_of], axis=1).astype(jnp.int32)

    stat_shape = ((2, 8, width), f32)
    acc_shape = ((2, HEAD, width), f32)
    rows_scratch = pltpu.VMEM((2, width, HEAD), bf16)
    early, rest = [0] + order[:WINDOW], order[WINDOW:-1]
    state = call(
        functools.partial(fwd_kernel, True, False, len(early)), "attend", [acc_shape, stat_shape],
        (meta, queries, q_back) + tuple(kv[k] for k in early), [rows_scratch], 1,
    )
    o_own, o_back, stats = call(
        functools.partial(fwd_kernel, False, True, len(rest)), "attend",
        [((HEAD, width), f32), ((HEAD, width), bf16), stat_shape],
        (meta, queries, q_back, output_gradient, g_back) + tuple(kv[k] for k in rest) + tuple(state),
        [rows_scratch, rows_scratch, pltpu.VMEM(*acc_shape)], 1,
    )

    far_own = shift(stats[1], "dp", -1)
    far_back = shift(stats[0], "dp", 1)

    operands = (meta, queries, q_back, output_gradient, g_back, stats, far_own, far_back)
    dq_own, dq_back, *pieces = call(
        functools.partial(bwd_kernel, True, True, n), "backward",
        [((tok, cols), f32), ((tok, cols), bf16)] + [piece_shape] * n,
        operands + tuple(kv[k] for k in order), [rows_scratch] * 2 + [pltpu.VMEM(*acc_shape)], 1,
    )
    both = jnp.concatenate([o_back.reshape(tok, cols), dq_back], axis=0)
    back, both = exchange(dict(zip(order, pieces)), order, -1, both, -1)
    attended, grad_queries, grad_kv = call(
        functools.partial(finish_kernel, "tensor"), "finish",
        [((tok, cols), bf16)] * 2 + [((n_img, part_keys, store_cols), bf16)],
        (o_own, stats, far_own, dq_own, both) + tuple(back[k] for k in range(n)),
    )
    return attended, grad_queries, grad_kv


def solution(mesh):
    return jax.shard_map(
        local,
        mesh=mesh,
        in_specs=(P("dp", "tensor"), P("dp", "tensor", None), P("dp", "tensor"), P(), P(), P()),
        out_specs=(P("dp", "tensor"), P("dp", "tensor"), P("dp", "tensor", None)),
        check_vma=False,
    )
```

```python
import functools
import math

import jax
import jax.numpy as jnp
from jax import lax
from jax.experimental import pallas as pl
from jax.experimental.pallas import tpu as pltpu
from jax.sharding import PartitionSpec as P

HEAD = 128
IMG_DEV = 2
NEG_FILL = -1e30
BIG = 1e30
LOG2E = 1.4426950408889634
SCALE = HEAD ** (-0.5)
SCALE2 = SCALE * LOG2E
WINDOW = 5

NT = (((1,), (1,)), ((), ()))
TN = (((0,), (0,)), ((), ()))
NN = (((1,), (0,)), ((), ()))


def dot(a, b, dims):
    return lax.dot_general(a, b, dims, preferred_element_type=jnp.float32)


def shift(value, axis, steps):
    count = lax.axis_size(axis)
    pairs = [(source, (source + steps) % count) for source in range(count)]
    return lax.ppermute(value, axis, pairs)


def stack_heads(src_ref, dst_ref, slot):
    rows, cols = src_ref.shape
    for h in range(cols // HEAD):
        dst_ref[slot, h * rows : (h + 1) * rows, :] = src_ref[:, h * HEAD : (h + 1) * HEAD]


def visible_rows(start, rows, width):
    pos = lax.broadcasted_iota(jnp.int32, (1, width), 1) % rows
    return pos >= start


def load_rows(refs, dst_ref):
    for slot, ref in enumerate(refs):
        stack_heads(ref, dst_ref, slot)


def split_kernel(axis, queries, cots, store, both, *pieces):
    n, width = len(pieces), pieces[0].shape[-1]
    tok = queries.shape[0]
    both[:tok, :] = queries[...]
    both[tok:, :] = cots[...]
    for k, piece in enumerate(pieces):
        col = lax.rem(lax.axis_index(axis) + k, n) * width
        piece[...] = store[:, :, pl.ds(pl.multiple_of(col, width), width)]


def fwd_kernel(first, last, blocks, *refs):
    refs = list(refs)
    meta, q_own, q_back = refs[:3]
    del refs[:3]
    if last:
        g_own, g_back = refs[:2]
        del refs[:2]
    kvs = refs[:blocks]
    del refs[:blocks]
    if not first:
        acc_in, stats_in = refs[:2]
        del refs[:2]
    if last:
        o_own, o_back, stats, qr, gr, acc = refs
    else:
        acc, stats, qr = refs
    tok, cols = q_own.shape
    width = tok * cols // HEAD
    load_rows((q_own, q_back), qr)
    if first:
        acc[...] = jnp.zeros_like(acc)
        stats[...] = jnp.zeros_like(stats)
        for slot in range(2):
            stats[slot, 0:1, :] = jnp.full((1, width), NEG_FILL, jnp.float32)
    else:
        acc[...] = acc_in[...]
        stats[...] = stats_in[...]
    for img in range(IMG_DEV):
        slot = meta[img, 0]
        seen = visible_rows(meta[img, 1], tok, width)
        scores = [dot(kv[img, :, :HEAD], qr[slot], NT) for kv in kvs]
        top = functools.reduce(jnp.maximum, [jnp.max(s, axis=0, keepdims=True) for s in scores])
        total = jnp.zeros((1, width), jnp.float32)
        out = jnp.zeros((HEAD, width), jnp.float32)
        for kv, s in zip(kvs, scores):
            part = jnp.exp2((s - top) * SCALE2)
            total = total + jnp.sum(part, axis=0, keepdims=True)
            out = out + dot(kv[img, :, HEAD:], part.astype(jnp.bfloat16), TN)
        old_top = stats[slot, 0:1, :]
        top = jnp.where(seen, top, NEG_FILL)
        new_top = jnp.maximum(old_top, top)
        old_w = jnp.exp2((old_top - new_top) * SCALE2)
        new_w = jnp.where(seen, jnp.exp2((top - new_top) * SCALE2), 0.0)
        stats[slot, 0:1, :] = new_top
        stats[slot, 1:2, :] = stats[slot, 1:2, :] * old_w + total * new_w
        acc[slot] = acc[slot] * old_w + out * new_w
    if last:
        load_rows((g_own, g_back), gr)
        eye = (
            lax.broadcasted_iota(jnp.int32, (HEAD, HEAD), 0)
            == lax.broadcasted_iota(jnp.int32, (HEAD, HEAD), 1)
        ).astype(jnp.bfloat16)
        for slot in range(2):
            total = stats[slot, 1:2, :]
            mean = acc[slot] * jnp.where(total > 0.0, 1.0 / jnp.maximum(total, 1e-30), 0.0)
            cot = dot(eye, gr[slot], NT)
            stats[slot, 2:3, :] = jnp.sum(cot * mean, axis=0, keepdims=True)
            if slot == 0:
                o_own[...] = mean
            else:
                o_back[...] = mean.astype(jnp.bfloat16)


def merge(first, second):
    top = jnp.maximum(first[0:1], second[0:1])
    w_first = first[1:2] * jnp.exp2((first[0:1] - top) * SCALE2)
    w_second = second[1:2] * jnp.exp2((second[0:1] - top) * SCALE2)
    total = w_first + w_second
    inv = jnp.where(total > 0.0, 1.0 / jnp.maximum(total, 1e-30), 0.0)
    return top, total, w_first * inv, w_second * inv


def bwd_kernel(first, last, blocks, *refs):
    refs = list(refs)
    meta, q_own, q_back, g_own, g_back, stats, far_own, far_back = refs[:8]
    del refs[:8]
    kvs = refs[:blocks]
    del refs[:blocks]
    if not first:
        acc_in = refs.pop(0)
    if last:
        dq_own, dq_back = refs[:2]
        del refs[:2]
    else:
        acc = refs.pop(0)
    dkvs = refs[:blocks]
    del refs[:blocks]
    if last:
        qr, gr, acc = refs
    else:
        qr, gr = refs
    tok, cols = q_own.shape
    width = tok * cols // HEAD
    load_rows((q_own, q_back), qr)
    load_rows((g_own, g_back), gr)
    acc[...] = jnp.zeros_like(acc) if first else acc_in[...]
    logs, deltas = [], []
    for slot, far in ((0, far_own), (1, far_back)):
        near_v = stats[slot]
        far_v = far[...]
        top, total, w_near, w_far = merge(near_v, far_v)
        logs.append(jnp.where(total > 0.0, top * SCALE2 + jnp.log(jnp.maximum(total, 1e-30)) * LOG2E, 0.0))
        deltas.append(w_near * near_v[2:3] + w_far * far_v[2:3])
    for img in range(IMG_DEV):
        slot = meta[img, 0]
        seen = visible_rows(meta[img, 1], tok, width)
        log_total = jnp.where(slot == 0, logs[0], logs[1])
        log_total = jnp.where(seen, log_total, BIG)
        delta = jnp.where(slot == 0, deltas[0], deltas[1])
        for kv, dkv in zip(kvs, dkvs):
            key = kv[img, :, :HEAD]
            part = jnp.exp2(dot(key, qr[slot], NT) * SCALE2 - log_total)
            dweight = dot(kv[img, :, HEAD:], gr[slot], NT)
            ds = (part * (dweight - delta)).astype(jnp.bfloat16)
            dkv[img, :, HEAD:] = dot(part.astype(jnp.bfloat16), gr[slot], NN).astype(jnp.bfloat16)
            dkv[img, :, :HEAD] = (dot(ds, qr[slot], NN) * SCALE).astype(jnp.bfloat16)
            acc[slot] = acc[slot] + dot(key, ds, TN)
    if last:
        for slot, out in ((0, dq_own), (1, dq_back)):
            for h in range(cols // HEAD):
                block = acc[slot, :, h * tok : (h + 1) * tok] * SCALE
                out[:, h * HEAD : (h + 1) * HEAD] = block.T.astype(out.dtype)


def finish_kernel(axis, o_own, stats, far, dq_own, both, *refs):
    pieces, (out, dq, dkv) = refs[:-3], refs[-3:]
    tok, cols = out.shape
    n, pair = len(pieces), pieces[0].shape[-1]
    for k, piece in enumerate(pieces):
        col = lax.rem(lax.axis_index(axis) + k, n) * pair
        dkv[:, :, pl.ds(pl.multiple_of(col, pair), pair)] = piece[...]
    _, _, w_near, w_far = merge(stats[0], far[...])
    for h in range(cols // HEAD):
        rows = slice(h * tok, (h + 1) * tok)
        whole = o_own[:, rows] * w_near[:, rows] + both[:tok, rows].astype(jnp.float32) * w_far[:, rows]
        out[:, h * HEAD : (h + 1) * HEAD] = whole.T.astype(out.dtype)
    dq[...] = (dq_own[...] + both[tok:, :].astype(jnp.float32)).astype(dq.dtype)


VMEM = pl.BlockSpec(memory_space=pltpu.VMEM)
SMEM = pl.BlockSpec(memory_space=pltpu.SMEM)


def call(kernel, name, outs, operands, scratch=(), smem=0, flops=0, aliases=None):
    return pl.pallas_call(
        kernel,
        out_shape=[jax.ShapeDtypeStruct(*o) for o in outs],
        in_specs=[SMEM] * smem + [VMEM] * (len(operands) - smem),
        out_specs=[VMEM] * len(outs),
        scratch_shapes=list(scratch),
        compiler_params=pltpu.CompilerParams(vmem_limit_bytes=32 * 1024 * 1024),
        cost_estimate=pl.CostEstimate(flops=flops, bytes_accessed=1 << 20, transcendentals=0),
        input_output_aliases=aliases or {},
        name=name,
    )(*operands)


def after(value, *others):
    return lax.optimization_barrier((value, *others))[0]


def within(value, steps):
    count = lax.axis_size("dp")
    half = count // 2
    inside = [(s, s + steps) for s in range(count) if s // half == (s + steps) // half and s + steps >= 0]
    return lax.ppermute(value, "dp", inside)


def seam_legs(steps):
    count, n = lax.axis_size("dp"), lax.axis_size("tensor")
    half = count // 2
    source, near = (half - 1, 0) if steps > 0 else (0, half - 1)
    relays = [5, 17, 25, 7, 29, 23, 3, 9] if half == 32 and n == 8 else [half - 1] * n

    def send(part, pairs):
        return lax.ppermute(part, ("dp", "tensor"), [(d * n + t, e * n + t) for d, e, t in pairs])

    fan = [(source + base, relays[t] + base, t) for base in (0, half) for t in range(n)]
    over = [(relays[t] + base, near + half - base, t) for base in (0, half) for t in range(n)]
    return lambda part: send(part, fan), lambda part: send(part, over)


def exchange(pieces, order, sign, both, steps):
    half = lax.axis_size("dp") // 2
    near = 0 if steps > 0 else half - 1
    first_leg, second_leg = seam_legs(steps)
    got = {}
    for i, k in enumerate(order):
        piece = after(pieces[k], got[order[i - WINDOW]]) if i >= WINDOW else pieces[k]
        got[k] = shift(piece, "tensor", sign * k) if k else piece
    over = second_leg(first_leg(both))
    both = jnp.where(lax.axis_index("dp") % half == near, over, within(both, steps))
    return got, both


def local(queries, key_value_store, output_gradient, image_ids, image_counts, image_start):
    bf16, f32 = jnp.bfloat16, jnp.float32
    tok, cols = queries.shape
    width = tok * cols // HEAD
    n = lax.axis_size("tensor")
    n_dp = lax.axis_size("dp")
    me_d = lax.axis_index("dp")
    n_img, part_keys, store_cols = key_value_store.shape
    pair = store_cols // n
    piece_shape = ((n_img, part_keys, pair), bf16)

    both, *sends = call(
        functools.partial(split_kernel, "tensor"), "split", [((2 * tok, cols), bf16)] + [piece_shape] * n,
        (queries, output_gradient, key_value_store),
    )
    order = [1, n - 1, n // 2] + [k for d in range(2, n // 2) for k in (d, n - d)] + [0]
    kv, both = exchange(sends, order, 1, both, 1)
    q_back, g_back = both[:tok], both[tok:]

    mine = me_d * IMG_DEV + jnp.arange(IMG_DEV, dtype=jnp.int32)
    rows = []
    for slot in range(2):
        sample = (me_d - slot) % n_dp
        ids, starts = image_ids[sample], image_start[sample]
        live = jnp.arange(ids.shape[0], dtype=jnp.int32) < image_counts[sample]
        hit = (ids[None, :] == mine[:, None]) & live[None, :]
        rows.append((jnp.any(hit, axis=1), jnp.sum(jnp.where(hit, starts[None, :], 0), axis=1)))
    slot_of = jnp.where(rows[0][0], 0, 1)
    start_of = jnp.where(rows[0][0], rows[0][1], rows[1][1])
    meta = jnp.stack([slot_of, start_of], axis=1).astype(jnp.int32)

    stat_shape = ((2, 8, width), f32)
    acc_shape = ((2, HEAD, width), f32)
    rows_scratch = pltpu.VMEM((2, width, HEAD), bf16)
    early, rest = [0] + order[:WINDOW], order[WINDOW:-1]
    state = call(
        functools.partial(fwd_kernel, True, False, len(early)), "attend", [acc_shape, stat_shape],
        (meta, queries, q_back) + tuple(kv[k] for k in early), [rows_scratch], 1,
    )
    o_own, o_back, stats = call(
        functools.partial(fwd_kernel, False, True, len(rest)), "attend",
        [((HEAD, width), f32), ((HEAD, width), bf16), stat_shape],
        (meta, queries, q_back, output_gradient, g_back) + tuple(kv[k] for k in rest) + tuple(state),
        [rows_scratch, rows_scratch, pltpu.VMEM(*acc_shape)], 1,
    )

    far_own = shift(stats[1], "dp", -1)
    far_back = shift(stats[0], "dp", 1)

    operands = (meta, queries, q_back, output_gradient, g_back, stats, far_own, far_back)
    dq_own, dq_back, *pieces = call(
        functools.partial(bwd_kernel, True, True, n), "backward",
        [((tok, cols), f32), ((tok, cols), bf16)] + [piece_shape] * n,
        operands + tuple(kv[k] for k in order), [rows_scratch] * 2 + [pltpu.VMEM(*acc_shape)], 1,
    )
    both = jnp.concatenate([o_back.reshape(tok, cols), dq_back], axis=0)
    back, both = exchange(dict(zip(order, pieces)), order, -1, both, -1)
    attended, grad_queries, grad_kv = call(
        functools.partial(finish_kernel, "tensor"), "finish",
        [((tok, cols), bf16)] * 2 + [((n_img, part_keys, store_cols), bf16)],
        (o_own, stats, far_own, dq_own, both) + tuple(back[k] for k in range(n)),
    )
    return attended, grad_queries, grad_kv


def solution(mesh):
    return jax.shard_map(
        local,
        mesh=mesh,
        in_specs=(P("dp", "tensor"), P("dp", "tensor", None), P("dp", "tensor"), P(), P(), P()),
        out_specs=(P("dp", "tensor"), P("dp", "tensor"), P("dp", "tensor", None)),
        check_vma=False,
    )
```

```python
import functools
import math

import jax
import jax.numpy as jnp
from jax import lax
from jax.experimental import pallas as pl
from jax.experimental.pallas import tpu as pltpu
from jax.sharding import PartitionSpec as P

HEAD = 128
IMG_DEV = 2
NEG_FILL = -1e30
BIG = 1e30
LOG2E = 1.4426950408889634
SCALE = HEAD ** (-0.5)
SCALE2 = SCALE * LOG2E
WINDOW = 5

NT = (((1,), (1,)), ((), ()))
TN = (((0,), (0,)), ((), ()))
NN = (((1,), (0,)), ((), ()))


def dot(a, b, dims):
    return lax.dot_general(a, b, dims, preferred_element_type=jnp.float32)


def shift(value, axis, steps):
    count = lax.axis_size(axis)
    pairs = [(source, (source + steps) % count) for source in range(count)]
    return lax.ppermute(value, axis, pairs)


def stack_heads(src_ref, dst_ref, slot):
    rows, cols = src_ref.shape
    for h in range(cols // HEAD):
        dst_ref[slot, h * rows : (h + 1) * rows, :] = src_ref[:, h * HEAD : (h + 1) * HEAD]


def visible_rows(start, rows, width):
    pos = lax.broadcasted_iota(jnp.int32, (1, width), 1) % rows
    return pos >= start


def load_rows(refs, dst_ref):
    for slot, ref in enumerate(refs):
        stack_heads(ref, dst_ref, slot)


def split_kernel(axis, queries, cots, store, both, *pieces):
    n, width = len(pieces), pieces[0].shape[-1]
    tok = queries.shape[0]
    both[:tok, :] = queries[...]
    both[tok:, :] = cots[...]
    for k, piece in enumerate(pieces):
        col = lax.rem(lax.axis_index(axis) + k, n) * width
        piece[...] = store[:, :, pl.ds(pl.multiple_of(col, width), width)]


def fwd_kernel(first, last, blocks, *refs):
    refs = list(refs)
    meta, q_own, q_back = refs[:3]
    del refs[:3]
    if last:
        g_own, g_back = refs[:2]
        del refs[:2]
    kvs = refs[:blocks]
    del refs[:blocks]
    if not first:
        acc_in, stats_in = refs[:2]
        del refs[:2]
    if last:
        o_own, o_back, stats, qr, gr, acc = refs
    else:
        acc, stats, qr = refs
    tok, cols = q_own.shape
    width = tok * cols // HEAD
    load_rows((q_own, q_back), qr)
    if first:
        acc[...] = jnp.zeros_like(acc)
        stats[...] = jnp.zeros_like(stats)
        for slot in range(2):
            stats[slot, 0:1, :] = jnp.full((1, width), NEG_FILL, jnp.float32)
    else:
        acc[...] = acc_in[...]
        stats[...] = stats_in[...]
    for img in range(IMG_DEV):
        slot = meta[img, 0]
        seen = visible_rows(meta[img, 1], tok, width)
        scores = [dot(kv[img, :, :HEAD], qr[slot], NT) for kv in kvs]
        top = functools.reduce(jnp.maximum, [jnp.max(s, axis=0, keepdims=True) for s in scores])
        total = jnp.zeros((1, width), jnp.float32)
        out = jnp.zeros((HEAD, width), jnp.float32)
        for kv, s in zip(kvs, scores):
            part = jnp.exp2((s - top) * SCALE2)
            total = total + jnp.sum(part, axis=0, keepdims=True)
            out = out + dot(kv[img, :, HEAD:], part.astype(jnp.bfloat16), TN)
        old_top = stats[slot, 0:1, :]
        top = jnp.where(seen, top, NEG_FILL)
        new_top = jnp.maximum(old_top, top)
        old_w = jnp.exp2((old_top - new_top) * SCALE2)
        new_w = jnp.where(seen, jnp.exp2((top - new_top) * SCALE2), 0.0)
        stats[slot, 0:1, :] = new_top
        stats[slot, 1:2, :] = stats[slot, 1:2, :] * old_w + total * new_w
        acc[slot] = acc[slot] * old_w + out * new_w
    if last:
        load_rows((g_own, g_back), gr)
        eye = (
            lax.broadcasted_iota(jnp.int32, (HEAD, HEAD), 0)
            == lax.broadcasted_iota(jnp.int32, (HEAD, HEAD), 1)
        ).astype(jnp.bfloat16)
        for slot in range(2):
            total = stats[slot, 1:2, :]
            mean = acc[slot] * jnp.where(total > 0.0, 1.0 / jnp.maximum(total, 1e-30), 0.0)
            cot = dot(eye, gr[slot], NT)
            stats[slot, 2:3, :] = jnp.sum(cot * mean, axis=0, keepdims=True)
            if slot == 0:
                o_own[...] = mean
            else:
                o_back[...] = mean.astype(jnp.bfloat16)


def merge(first, second):
    top = jnp.maximum(first[0:1], second[0:1])
    w_first = first[1:2] * jnp.exp2((first[0:1] - top) * SCALE2)
    w_second = second[1:2] * jnp.exp2((second[0:1] - top) * SCALE2)
    total = w_first + w_second
    inv = jnp.where(total > 0.0, 1.0 / jnp.maximum(total, 1e-30), 0.0)
    return top, total, w_first * inv, w_second * inv


def bwd_kernel(first, last, blocks, *refs):
    refs = list(refs)
    meta, q_own, q_back, g_own, g_back, stats, far_own, far_back = refs[:8]
    del refs[:8]
    kvs = refs[:blocks]
    del refs[:blocks]
    if not first:
        acc_in = refs.pop(0)
    if last:
        dq_own, dq_back = refs[:2]
        del refs[:2]
    else:
        acc = refs.pop(0)
    dkvs = refs[:blocks]
    del refs[:blocks]
    if last:
        qr, gr, acc = refs
    else:
        qr, gr = refs
    tok, cols = q_own.shape
    width = tok * cols // HEAD
    load_rows((q_own, q_back), qr)
    load_rows((g_own, g_back), gr)
    acc[...] = jnp.zeros_like(acc) if first else acc_in[...]
    logs, deltas = [], []
    for slot, far in ((0, far_own), (1, far_back)):
        near_v = stats[slot]
        far_v = far[...]
        top, total, w_near, w_far = merge(near_v, far_v)
        logs.append(jnp.where(total > 0.0, top * SCALE2 + jnp.log(jnp.maximum(total, 1e-30)) * LOG2E, 0.0))
        deltas.append(w_near * near_v[2:3] + w_far * far_v[2:3])
    for img in range(IMG_DEV):
        slot = meta[img, 0]
        seen = visible_rows(meta[img, 1], tok, width)
        log_total = jnp.where(slot == 0, logs[0], logs[1])
        log_total = jnp.where(seen, log_total, BIG)
        delta = jnp.where(slot == 0, deltas[0], deltas[1])
        for kv, dkv in zip(kvs, dkvs):
            key = kv[img, :, :HEAD]
            part = jnp.exp2(dot(key, qr[slot], NT) * SCALE2 - log_total)
            dweight = dot(kv[img, :, HEAD:], gr[slot], NT)
            ds = (part * (dweight - delta)).astype(jnp.bfloat16)
            dkv[img, :, HEAD:] = dot(part.astype(jnp.bfloat16), gr[slot], NN).astype(jnp.bfloat16)
            dkv[img, :, :HEAD] = (dot(ds, qr[slot], NN) * SCALE).astype(jnp.bfloat16)
            acc[slot] = acc[slot] + dot(key, ds, TN)
    if last:
        for slot, out in ((0, dq_own), (1, dq_back)):
            for h in range(cols // HEAD):
                block = acc[slot, :, h * tok : (h + 1) * tok] * SCALE
                out[:, h * HEAD : (h + 1) * HEAD] = block.T.astype(out.dtype)


def finish_kernel(axis, o_own, stats, far, dq_own, both, *refs):
    pieces, (out, dq, dkv) = refs[:-3], refs[-3:]
    tok, cols = out.shape
    n, pair = len(pieces), pieces[0].shape[-1]
    for k, piece in enumerate(pieces):
        col = lax.rem(lax.axis_index(axis) + k, n) * pair
        dkv[:, :, pl.ds(pl.multiple_of(col, pair), pair)] = piece[...]
    _, _, w_near, w_far = merge(stats[0], far[...])
    for h in range(cols // HEAD):
        rows = slice(h * tok, (h + 1) * tok)
        whole = o_own[:, rows] * w_near[:, rows] + both[:tok, rows].astype(jnp.float32) * w_far[:, rows]
        out[:, h * HEAD : (h + 1) * HEAD] = whole.T.astype(out.dtype)
    dq[...] = (dq_own[...] + both[tok:, :].astype(jnp.float32)).astype(dq.dtype)


VMEM = pl.BlockSpec(memory_space=pltpu.VMEM)
SMEM = pl.BlockSpec(memory_space=pltpu.SMEM)


def call(kernel, name, outs, operands, scratch=(), smem=0, flops=0, aliases=None):
    return pl.pallas_call(
        kernel,
        out_shape=[jax.ShapeDtypeStruct(*o) for o in outs],
        in_specs=[SMEM] * smem + [VMEM] * (len(operands) - smem),
        out_specs=[VMEM] * len(outs),
        scratch_shapes=list(scratch),
        compiler_params=pltpu.CompilerParams(vmem_limit_bytes=32 * 1024 * 1024),
        cost_estimate=pl.CostEstimate(flops=flops, bytes_accessed=1 << 20, transcendentals=0),
        input_output_aliases=aliases or {},
        name=name,
    )(*operands)


def after(value, *others):
    return lax.optimization_barrier((value, *others))[0]


def within(value, steps):
    count = lax.axis_size("dp")
    half = count // 2
    inside = [(s, s + steps) for s in range(count) if s // half == (s + steps) // half and s + steps >= 0]
    return lax.ppermute(value, "dp", inside)


def seam_legs(steps):
    count, n = lax.axis_size("dp"), lax.axis_size("tensor")
    half = count // 2
    source, near = (half - 1, 0) if steps > 0 else (0, half - 1)
    relays = [5, 17, 25, 7, 29, 23, 3, 9] if half == 32 and n == 8 else [half - 1] * n

    def send(part, pairs):
        return lax.ppermute(part, ("dp", "tensor"), [(d * n + t, e * n + t) for d, e, t in pairs])

    fan = [(source + base, relays[t] + base, t) for base in (0, half) for t in range(n)]
    over = [(relays[t] + base, near + half - base, t) for base in (0, half) for t in range(n)]
    return lambda part: send(part, fan), lambda part: send(part, over)


def exchange(pieces, order, sign, both, steps):
    half = lax.axis_size("dp") // 2
    near = 0 if steps > 0 else half - 1
    first_leg, second_leg = seam_legs(steps)
    got = {}
    for i, k in enumerate(order):
        piece = after(pieces[k], got[order[i - WINDOW]]) if i >= WINDOW else pieces[k]
        got[k] = shift(piece, "tensor", sign * k) if k else piece
    over = second_leg(first_leg(both))
    both = jnp.where(lax.axis_index("dp") % half == near, over, within(both, steps))
    return got, both


def local(queries, key_value_store, output_gradient, image_ids, image_counts, image_start):
    bf16, f32 = jnp.bfloat16, jnp.float32
    tok, cols = queries.shape
    width = tok * cols // HEAD
    n = lax.axis_size("tensor")
    n_dp = lax.axis_size("dp")
    me_d = lax.axis_index("dp")
    n_img, part_keys, store_cols = key_value_store.shape
    pair = store_cols // n
    piece_shape = ((n_img, part_keys, pair), bf16)

    both, *sends = call(
        functools.partial(split_kernel, "tensor"), "split", [((2 * tok, cols), bf16)] + [piece_shape] * n,
        (queries, output_gradient, key_value_store),
    )
    order = [1, n - 1, 2, n - 2, n // 2] + [k for d in range(3, n // 2) for k in (d, n - d)] + [0]
    kv, both = exchange(sends, order, 1, both, 1)
    q_back, g_back = both[:tok], both[tok:]

    mine = me_d * IMG_DEV + jnp.arange(IMG_DEV, dtype=jnp.int32)
    rows = []
    for slot in range(2):
        sample = (me_d - slot) % n_dp
        ids, starts = image_ids[sample], image_start[sample]
        live = jnp.arange(ids.shape[0], dtype=jnp.int32) < image_counts[sample]
        hit = (ids[None, :] == mine[:, None]) & live[None, :]
        rows.append((jnp.any(hit, axis=1), jnp.sum(jnp.where(hit, starts[None, :], 0), axis=1)))
    slot_of = jnp.where(rows[0][0], 0, 1)
    start_of = jnp.where(rows[0][0], rows[0][1], rows[1][1])
    meta = jnp.stack([slot_of, start_of], axis=1).astype(jnp.int32)

    stat_shape = ((2, 8, width), f32)
    acc_shape = ((2, HEAD, width), f32)
    rows_scratch = pltpu.VMEM((2, width, HEAD), bf16)
    early, rest = [0] + order[:WINDOW], order[WINDOW:-1]
    state = call(
        functools.partial(fwd_kernel, True, False, len(early)), "attend", [acc_shape, stat_shape],
        (meta, queries, q_back) + tuple(kv[k] for k in early), [rows_scratch], 1,
    )
    o_own, o_back, stats = call(
        functools.partial(fwd_kernel, False, True, len(rest)), "attend",
        [((HEAD, width), f32), ((HEAD, width), bf16), stat_shape],
        (meta, queries, q_back, output_gradient, g_back) + tuple(kv[k] for k in rest) + tuple(state),
        [rows_scratch, rows_scratch, pltpu.VMEM(*acc_shape)], 1,
    )

    far_own = shift(stats[1], "dp", -1)
    far_back = shift(stats[0], "dp", 1)

    operands = (meta, queries, q_back, output_gradient, g_back, stats, far_own, far_back)
    dq_own, dq_back, *pieces = call(
        functools.partial(bwd_kernel, True, True, n), "backward",
        [((tok, cols), f32), ((tok, cols), bf16)] + [piece_shape] * n,
        operands + tuple(kv[k] for k in order), [rows_scratch] * 2 + [pltpu.VMEM(*acc_shape)], 1,
    )
    both = jnp.concatenate([o_back.reshape(tok, cols), dq_back], axis=0)
    back, both = exchange(dict(zip(order, pieces)), order, -1, both, -1)
    attended, grad_queries, grad_kv = call(
        functools.partial(finish_kernel, "tensor"), "finish",
        [((tok, cols), bf16)] * 2 + [((n_img, part_keys, store_cols), bf16)],
        (o_own, stats, far_own, dq_own, both) + tuple(back[k] for k in range(n)),
    )
    return attended, grad_queries, grad_kv


def solution(mesh):
    return jax.shard_map(
        local,
        mesh=mesh,
        in_specs=(P("dp", "tensor"), P("dp", "tensor", None), P("dp", "tensor"), P(), P(), P()),
        out_specs=(P("dp", "tensor"), P("dp", "tensor"), P("dp", "tensor", None)),
        check_vma=False,
    )
```
